32 devices in a mesh: section: 4 (over y, core), dp: 8 (over z, x).
Axes of the slice: x: 2, y: 2, z: 4, core: 2. Of those that a mesh axis runs over, the one named last changes fastest.
Arguments:
- inputs: bfloat16 [1280, 2560], P('dp'), may hold values from -6 to 6
- cotangent: bfloat16 [1280, 2560], P('dp'), may hold values from -6 to 6
- weights: bfloat16 [4, 2560, 2560], P('section', 'dp'), may hold values from -0.0625 to 0.0625
- lengths: int32 [40], P('dp'), may hold values from 1 to 32, as said below
Outputs:
- pre_inputs: bfloat16 [4, 1280, 2560], P('section', 'dp')
- pre_grads: bfloat16 [4, 1280, 2560], P('section', 'dp')
The draws below stay inside these ranges and needn't reach their ends.
Inputs may be any that keep to these rules, and one draw needn't show every extreme that they name: `lengths`: each micro-batch has at least one live token; some micro-batch is full and some has exactly one.
All inputs are finite; a program needn't handle non-finite values.
Results may differ from the reference program's by a relative error of at most 0.012.
Values may be sent and summed in bfloat16 or wider, within the bound.
A program may use at most 64 MiB of HBM per device.

```python
import jax
import jax.numpy as jnp
from jax import lax

D = 2560
BLOCK = 160
MB = 32
TOKENS = 1280
SECTIONS = 4


def draw_lengths(key, part):
    base = jax.random.randint(key, (TOKENS // MB,), 1, MB + 1)
    base = base.at[0].set(MB)
    return base.at[-1].set(1).astype(jnp.int32)


def block_levels(rng, extent, cuts, least, largest):
    factor_of = 1.0
    for dim, shards_of in cuts:
        heights = jax.random.uniform(jax.random.fold_in(jax.random.fold_in(rng, 6), dim), (shards_of,), jnp.float32, least / len(cuts), largest / len(cuts))
        factor_of = factor_of * jnp.repeat(jnp.exp(heights), extent[dim] // shards_of).reshape((-1,) + (1,) * (len(extent) - 1 - dim))
    return factor_of


def normal_values(key, dims, spread, bound, split=(), held_as=jnp.bfloat16):
    gain = block_levels(key, dims, split, -0.22, 0.18) if split else 1.0
    values = jax.random.normal(key, dims, jnp.float32) * spread * gain
    return jnp.minimum(jnp.maximum(values, -bound), bound).astype(held_as)


def setup_inputs(seed: int = 0) -> dict:
    seeds = jax.random.split(jax.random.key(seed), 5)
    return {
        "inputs": normal_values(seeds[0], (TOKENS, D), 1.0, 6.0, ((0, 8),)),
        "cotangent": normal_values(seeds[1], (TOKENS, D), 1.0, 6.0, ((0, 8),)),
        "weights": normal_values(seeds[2], (SECTIONS, D, D), (4 * D) ** -0.5, 0.0625, ((0, 4), (1, 8))),
        "lengths": draw_lengths(jax.random.fold_in(seeds[4], 71), 0),
    }


epsilon = 1e-05
damping = 0.1

def normalize(hidden):
    wide = hidden.astype(jnp.float32)
    factor = lax.rsqrt(lax.optimization_barrier(jnp.mean(wide * wide, axis=-1, keepdims=True)) + epsilon)
    return (wide * factor, factor)

def invert_blocks(blocks, counted):
    order = blocks.shape[-1]
    identity = jnp.eye(order, dtype=jnp.float32)
    damped = blocks / counted + damping * identity
    lower = jnp.linalg.cholesky(damped)
    half_way = lax.linalg.triangular_solve(lower, jnp.broadcast_to(identity, damped.shape), left_side=True, lower=True)
    inverse = lax.linalg.triangular_solve(lower, half_way, left_side=True, lower=True, transpose_a=True)
    return inverse.astype(jnp.bfloat16)

def gram_blocks(values, live):
    masked = jnp.where(live, values, jnp.zeros((), values.dtype)).astype(jnp.float32)
    shaped = masked.reshape(values.shape[0], D // BLOCK, BLOCK)
    return jnp.einsum('tbi,tbj->bij', shaped, shaped, precision=lax.Precision.HIGHEST)

def apply_blocks(values, inverse):
    shaped = values.astype(jnp.float32).reshape(values.shape[0], D // BLOCK, BLOCK)
    result = jnp.einsum('tbi,bij->tbj', shaped, inverse.astype(jnp.float32), precision=lax.Precision.HIGHEST)
    return result.reshape(values.shape[0], D).astype(jnp.bfloat16)

def reference(inputs, cotangent, weights, lengths):
    hidden = inputs
    hiddens = []
    activations = []
    for layer in range(SECTIONS):
        hiddens.append(hidden)
        normed, factor = normalize(hidden)
        activation = normed.astype(jnp.bfloat16)
        activations.append(activation)
        hidden = (hidden.astype(jnp.float32) + jnp.dot(activation.astype(jnp.float32), weights[layer].astype(jnp.float32), preferred_element_type=jnp.float32)).astype(jnp.bfloat16)
    gradients = [None] * SECTIONS
    current = cotangent
    for layer in range(SECTIONS - 1, -1, -1):
        gradients[layer] = current
        if layer > 0:
            normed, factor = normalize(hiddens[layer])
            back = jnp.dot(current.astype(jnp.float32), weights[layer].T.astype(jnp.float32), preferred_element_type=jnp.float32)
            through = factor * (back - normed * lax.optimization_barrier(jnp.mean(back * normed, axis=-1, keepdims=True)))
            current = (current.astype(jnp.float32) + through).astype(jnp.bfloat16)
    live = (jnp.arange(MB)[None, :] < lengths[:, None]).reshape(TOKENS, 1)
    counted = jnp.sum(live.astype(jnp.float32))
    first_out = []
    second_out = []
    for layer in range(SECTIONS):
        inverse_a = invert_blocks(gram_blocks(activations[layer], live), counted)
        inverse_g = invert_blocks(gram_blocks(gradients[layer], live), counted)
        first_out.append(apply_blocks(activations[layer], inverse_a))
        second_out.append(apply_blocks(gradients[layer], inverse_g))
    return (jnp.stack(first_out), jnp.stack(second_out))
```

```python
import functools

import jax
import jax.numpy as jnp
from jax import lax
from jax.experimental import pallas as pl
from jax.experimental.pallas import tpu as pltpu
from jax.sharding import PartitionSpec as P

BLOCK = 160
PANEL = 32
LANES = 128
PACK = LANES // PANEL

epsilon = 1e-05
damping = 0.1

exact_dot = functools.partial(
    lax.dot_general, precision=lax.Precision.HIGHEST, preferred_element_type=jnp.float32
)


def normalize(hidden):
    wide = hidden.astype(jnp.float32)
    factor = lax.rsqrt(jnp.mean(wide * wide, axis=-1, keepdims=True) + epsilon)
    return (wide * factor, factor)


def sweep_panel(panel, width):
    rows = lax.broadcasted_iota(jnp.int32, (PANEL, width), 0)
    lanes = lax.broadcasted_iota(jnp.int32, (PANEL, width), 1)
    within = lanes % PANEL
    base = lanes - within
    for k in range(PANEL):
        column = jnp.take_along_axis(panel, base + k, axis=1)
        row = jnp.broadcast_to(panel[k : k + 1, :], (PANEL, width))
        pivot = jnp.broadcast_to(column[k : k + 1, :], (PANEL, width))
        inverse = 1.0 / pivot
        scaled = row * inverse
        inner = panel - column * scaled
        inner = jnp.where(within == k, column * inverse, inner)
        edge = jnp.where(within == k, -inverse, scaled)
        panel = jnp.where(rows == k, edge, inner)
    return panel


def invert_in_place(work, packed, count):
    for start in range(0, count, PACK):
        members = range(start, min(count, start + PACK))
        for k in range(BLOCK // PANEL):
            at = slice(k * PANEL, (k + 1) * PANEL)
            packed[...] = jnp.zeros_like(packed)
            for m in members:
                packed[:, (m - start) * PANEL : (m - start + 1) * PANEL] = work[m, at, at]
            packed[...] = sweep_panel(packed[...], LANES)
            for m in members:
                inverse = -packed[:, (m - start) * PANEL : (m - start + 1) * PANEL]
                row = work[m, at, :]
                across = exact_dot(inverse, row, (((1,), (0,)), ((), ())))
                down = exact_dot(row, inverse, (((0,), (0,)), ((), ())))
                work[m] = work[m] - exact_dot(row, across, (((0,), (0,)), ((), ())))
                work[m, at, :] = across
                work[m, :, at] = down
                work[m, at, at] = -inverse


def invert_kernel(count, counted_ref, blocks_ref, out_ref, work, packed):
    scale = 1.0 / counted_ref[0, 0]
    diagonal = lax.broadcasted_iota(jnp.int32, (BLOCK, BLOCK), 0) == lax.broadcasted_iota(
        jnp.int32, (BLOCK, BLOCK), 1
    )
    for m in range(count):
        work[m] = blocks_ref[m] * scale + jnp.where(diagonal, damping, 0.0)
    invert_in_place(work, packed, count)
    for m in range(count):
        out_ref[m] = (-work[m]).astype(jnp.bfloat16)


def invert_blocks(blocks, counted):
    count = blocks.shape[0]
    return pl.pallas_call(
        functools.partial(invert_kernel, count),
        out_shape=jax.ShapeDtypeStruct(blocks.shape, jnp.bfloat16),
        in_specs=[
            pl.BlockSpec(memory_space=pltpu.SMEM),
            pl.BlockSpec(memory_space=pltpu.VMEM),
        ],
        out_specs=pl.BlockSpec(memory_space=pltpu.VMEM),
        scratch_shapes=[
            pltpu.VMEM(blocks.shape, jnp.float32),
            pltpu.VMEM((PANEL, LANES), jnp.float32),
        ],
        compiler_params=pltpu.CompilerParams(vmem_limit_bytes=32 * 1024 * 1024),
    )(counted.reshape(1, 1), blocks)


def apply_blocks(values, inverse):
    shaped = values.reshape(values.shape[0], inverse.shape[0], inverse.shape[1])
    result = jnp.einsum("tbi,bij->tbj", shaped, inverse, preferred_element_type=jnp.float32)
    return result.reshape(1, values.shape[0], values.shape[1]).astype(jnp.bfloat16)


def on_device(inputs, cotangent, weights, lengths):
    section_index = lax.axis_index("section")
    section_count = lax.axis_size("section")
    token_count, width = inputs.shape
    micro_count = lengths.shape[0]
    batch_rows = token_count // micro_count
    live = (jnp.arange(batch_rows)[None, :] < lengths[:, None]).reshape(token_count, 1)
    counted = lax.psum(jnp.sum(live.astype(jnp.float32)), "dp")
    full_weight = lax.all_gather(weights, "dp", axis=1, tiled=True)[0]

    hidden = inputs
    for stage in range(section_count - 1):
        activation = normalize(hidden)[0].astype(jnp.bfloat16)
        result = (
            hidden.astype(jnp.float32)
            + jnp.dot(activation, full_weight, preferred_element_type=jnp.float32)
        ).astype(jnp.bfloat16)
        arrived = lax.ppermute(result, "section", [(stage, stage + 1)])
        hidden = jnp.where(section_index == stage + 1, arrived, hidden)

    normed, factor = normalize(hidden)
    activations = normed.astype(jnp.bfloat16)
    gradients = cotangent
    for stage in range(section_count - 1, 0, -1):
        back = lax.dot_general(
            gradients, full_weight, (((1,), (1,)), ((), ())), preferred_element_type=jnp.float32
        )
        through = factor * (back - normed * jnp.mean(back * normed, axis=-1, keepdims=True))
        result = (gradients.astype(jnp.float32) + through).astype(jnp.bfloat16)
        arrived = lax.ppermute(result, "section", [(stage, stage - 1)])
        gradients = jnp.where(section_index == stage - 1, arrived, gradients)

    blocks_each = width // BLOCK
    zero_value = jnp.zeros((), jnp.bfloat16)
    masked_act = jnp.where(live, activations, zero_value).reshape(token_count, blocks_each, BLOCK)
    masked_grad = jnp.where(live, gradients, zero_value).reshape(token_count, blocks_each, BLOCK)
    gram_act = jnp.einsum(
        "tbi,tbj->bij", masked_act, masked_act, preferred_element_type=jnp.float32
    )
    gram_grad = jnp.einsum(
        "tbi,tbj->bij", masked_grad, masked_grad, preferred_element_type=jnp.float32
    )
    stacked = jnp.concatenate([gram_act, gram_grad], axis=0)
    owned = lax.psum_scatter(stacked, "dp", scatter_dimension=0, tiled=True)
    inverses = lax.all_gather(invert_blocks(owned, counted), "dp", axis=0, tiled=True)
    pre_inputs = apply_blocks(activations, inverses[:blocks_each])
    pre_grads = apply_blocks(gradients, inverses[blocks_each:])
    return (pre_inputs, pre_grads)


def solution(mesh):
    in_specs = (P("dp", None), P("dp", None), P("section", "dp", None), P("dp"))
    out_specs = (P("section", "dp", None), P("section", "dp", None))
    return jax.shard_map(
        on_device, mesh=mesh, in_specs=in_specs, out_specs=out_specs, check_vma=False
    )
```

```python
import functools

import jax
import jax.numpy as jnp
from jax import lax
from jax.experimental import pallas as pl
from jax.experimental.pallas import tpu as pltpu
from jax.sharding import PartitionSpec as P

BLOCK = 160
PANEL = 32
LANES = 128
PACK = LANES // PANEL

epsilon = 1e-05
damping = 0.1

exact_dot = functools.partial(
    lax.dot_general, precision=lax.Precision.HIGHEST, preferred_element_type=jnp.float32
)


def normalize(hidden):
    wide = hidden.astype(jnp.float32)
    factor = lax.rsqrt(jnp.mean(wide * wide, axis=-1, keepdims=True) + epsilon)
    return (wide * factor, factor)


def sweep_panel(panel, width):
    rows = lax.broadcasted_iota(jnp.int32, (PANEL, width), 0)
    lanes = lax.broadcasted_iota(jnp.int32, (PANEL, width), 1)
    within = lanes % PANEL
    base = lanes - within
    for k in range(PANEL):
        column = jnp.take_along_axis(panel, base + k, axis=1)
        row = jnp.broadcast_to(panel[k : k + 1, :], (PANEL, width))
        pivot = jnp.broadcast_to(column[k : k + 1, :], (PANEL, width))
        inverse = 1.0 / pivot
        scaled = row * inverse
        inner = panel - column * scaled
        inner = jnp.where(within == k, column * inverse, inner)
        edge = jnp.where(within == k, -inverse, scaled)
        panel = jnp.where(rows == k, edge, inner)
    return panel


def invert_in_place(work, packed, count):
    for start in range(0, count, PACK):
        members = range(start, min(count, start + PACK))
        for k in range(BLOCK // PANEL):
            at = slice(k * PANEL, (k + 1) * PANEL)
            packed[...] = jnp.zeros_like(packed)
            for m in members:
                packed[:, (m - start) * PANEL : (m - start + 1) * PANEL] = work[m, at, at]
            packed[...] = sweep_panel(packed[...], LANES)
            for m in members:
                inverse = -packed[:, (m - start) * PANEL : (m - start + 1) * PANEL]
                row = work[m, at, :]
                across = exact_dot(inverse, row, (((1,), (0,)), ((), ())))
                down = exact_dot(row, inverse, (((0,), (0,)), ((), ())))
                work[m] = work[m] - exact_dot(row, across, (((0,), (0,)), ((), ())))
                work[m, at, :] = across
                work[m, :, at] = down
                work[m, at, at] = -inverse


def invert_kernel(count, blocks_ref, out_ref, work, packed):
    scale = 1.0 / blocks_ref[0, BLOCK : BLOCK + 1, :]
    diagonal = lax.broadcasted_iota(jnp.int32, (BLOCK, BLOCK), 0) == lax.broadcasted_iota(
        jnp.int32, (BLOCK, BLOCK), 1
    )
    for m in range(count):
        work[m] = blocks_ref[m, :BLOCK, :] * scale + jnp.where(diagonal, damping, 0.0)
    invert_in_place(work, packed, count)
    for m in range(count):
        out_ref[m] = (-work[m]).astype(jnp.bfloat16)


def invert_blocks(blocks):
    count = blocks.shape[0]
    shape = (count, BLOCK, BLOCK)
    return pl.pallas_call(
        functools.partial(invert_kernel, count),
        out_shape=jax.ShapeDtypeStruct(shape, jnp.bfloat16),
        in_specs=[pl.BlockSpec(memory_space=pltpu.VMEM)],
        out_specs=pl.BlockSpec(memory_space=pltpu.VMEM),
        scratch_shapes=[
            pltpu.VMEM(shape, jnp.float32),
            pltpu.VMEM((PANEL, LANES), jnp.float32),
        ],
        compiler_params=pltpu.CompilerParams(vmem_limit_bytes=32 * 1024 * 1024),
    )(blocks)


def ring_device(place, count):
    back = lax.div(place, count // 2)
    return (1 - back) * (2 * place) + back * (2 * (count - 1 - place) + 1)


def ring_place(index, count):
    back = lax.rem(index, 2)
    row = lax.div(index, 2)
    return (1 - back) * row + back * (count - 1 - row)


def ring_kernel(count, own_ref, out_ref, local_sem, send_sem, recv_sem):
    rows = own_ref.shape[0]
    first = rows // 32 * 16
    starts, sizes = (0, first), (first, rows - first)
    me = lax.axis_index("dp")
    place = ring_place(me, count)
    targets = [
        ring_device(lax.rem(place + 1, count), count),
        ring_device(lax.rem(place + count - 1, count), count),
    ]
    barrier = pltpu.get_barrier_semaphore()
    for target in targets:
        pl.semaphore_signal(
            barrier, inc=1, device_id={"dp": target}, device_id_type=pl.DeviceIdType.MESH
        )
    pl.semaphore_wait(barrier, 2)

    def part(owner, piece):
        return out_ref.at[pl.ds(pl.multiple_of(owner * rows + starts[piece], 16), sizes[piece])]

    own_copy = pltpu.make_async_copy(
        own_ref, out_ref.at[pl.ds(pl.multiple_of(me * rows, 16), rows)], local_sem
    )
    steps = count // 2
    copies = {}
    waited = set()
    for step in range(steps):
        for piece in range(2):
            for way in range(2):
                if step == steps - 1 and piece != way:
                    continue
                travelled = lax.rem(place + (count - step if way == 0 else step), count)
                owner = ring_device(travelled, count)
                if step == 0:
                    source = own_ref.at[pl.ds(starts[piece], sizes[piece])]
                else:
                    copies[step - 1, piece, way].wait_recv()
                    waited.add((step - 1, piece, way))
                    source = part(owner, piece)
                copy = pltpu.make_async_remote_copy(
                    src_ref=source,
                    dst_ref=part(owner, piece),
                    send_sem=send_sem.at[step, piece, way],
                    recv_sem=recv_sem.at[step, piece, way],
                    device_id={"dp": targets[way]},
                    device_id_type=pl.DeviceIdType.MESH,
                )
                copy.start()
                copies[step, piece, way] = copy
        if step == 0:
            own_copy.start()
    for key, copy in copies.items():
        if key not in waited:
            copy.wait_recv()
    for copy in copies.values():
        copy.wait_send()
    own_copy.wait()


def ring_gather(own, collective_id):
    count = lax.axis_size("dp")
    rows, columns = own.shape
    return pl.pallas_call(
        functools.partial(ring_kernel, count),
        out_shape=jax.ShapeDtypeStruct((count * rows, columns), own.dtype),
        in_specs=[pl.BlockSpec(memory_space=pl.ANY)],
        out_specs=pl.BlockSpec(memory_space=pl.ANY),
        scratch_shapes=[
            pltpu.SemaphoreType.DMA,
            pltpu.SemaphoreType.DMA((count // 2, 2, 2)),
            pltpu.SemaphoreType.DMA((count // 2, 2, 2)),
        ],
        compiler_params=pltpu.CompilerParams(collective_id=collective_id, has_side_effects=True),
    )(own)


def apply_blocks(values, inverse):
    shaped = values.reshape(values.shape[0], inverse.shape[0], inverse.shape[1])
    result = jnp.einsum("tbi,bij->tbj", shaped, inverse, preferred_element_type=jnp.float32)
    return result.reshape(1, values.shape[0], values.shape[1]).astype(jnp.bfloat16)


def on_device(inputs, cotangent, weights, lengths):
    section_index = lax.axis_index("section")
    section_count = lax.axis_size("section")
    token_count, width = inputs.shape
    micro_count = lengths.shape[0]
    batch_rows = token_count // micro_count
    live = (jnp.arange(batch_rows)[None, :] < lengths[:, None]).reshape(token_count, 1)
    counted = jnp.sum(live.astype(jnp.float32))
    full_weight = ring_gather(weights[0], 0)

    hidden = inputs
    for stage in range(section_count - 1):
        activation = normalize(hidden)[0].astype(jnp.bfloat16)
        result = (
            hidden.astype(jnp.float32)
            + jnp.dot(activation, full_weight, preferred_element_type=jnp.float32)
        ).astype(jnp.bfloat16)
        arrived = lax.ppermute(result, "section", [(stage, stage + 1)])
        hidden = jnp.where(section_index == stage + 1, arrived, hidden)

    normed, factor = normalize(hidden)
    activations = normed.astype(jnp.bfloat16)
    gradients = cotangent
    for stage in range(section_count - 1, 0, -1):
        back = lax.dot_general(
            gradients, full_weight, (((1,), (1,)), ((), ())), preferred_element_type=jnp.float32
        )
        through = factor * (back - normed * jnp.mean(back * normed, axis=-1, keepdims=True))
        result = (gradients.astype(jnp.float32) + through).astype(jnp.bfloat16)
        arrived = lax.ppermute(result, "section", [(stage, stage - 1)])
        gradients = jnp.where(section_index == stage - 1, arrived, gradients)

    blocks_each = width // BLOCK
    zero_value = jnp.zeros((), jnp.bfloat16)
    masked_act = jnp.where(live, activations, zero_value).reshape(token_count, blocks_each, BLOCK)
    masked_grad = jnp.where(live, gradients, zero_value).reshape(token_count, blocks_each, BLOCK)
    gram_act = jnp.einsum(
        "tbi,tbj->bij", masked_act, masked_act, preferred_element_type=jnp.float32
    )
    gram_grad = jnp.einsum(
        "tbi,tbj->bij", masked_grad, masked_grad, preferred_element_type=jnp.float32
    )
    stacked = jnp.concatenate([gram_act, gram_grad], axis=0)
    counts = jnp.full((stacked.shape[0], 8, BLOCK), counted, jnp.float32)
    stacked = jnp.concatenate([stacked, counts], axis=1)
    owned = lax.psum_scatter(stacked, "dp", scatter_dimension=0, tiled=True)
    inverse = invert_blocks(owned)
    inverses = ring_gather(inverse.reshape(-1, BLOCK), 1).reshape(-1, BLOCK, BLOCK)
    pre_inputs = apply_blocks(activations, inverses[:blocks_each])
    pre_grads = apply_blocks(gradients, inverses[blocks_each:])
    return (pre_inputs, pre_grads)


def solution(mesh):
    in_specs = (P("dp", None), P("dp", None), P("section", "dp", None), P("dp"))
    out_specs = (P("section", "dp", None), P("section", "dp", None))
    return jax.shard_map(
        on_device, mesh=mesh, in_specs=in_specs, out_specs=out_specs, check_vma=False
    )
```

```python
import functools

import jax
import jax.numpy as jnp
from jax import lax
from jax.experimental import pallas as pl
from jax.experimental.pallas import tpu as pltpu
from jax.sharding import PartitionSpec as P

BLOCK = 160
PANEL = 32
LANES = 128
PACK = LANES // PANEL

epsilon = 1e-05
damping = 0.1

exact_dot = functools.partial(
    lax.dot_general, precision=lax.Precision.HIGHEST, preferred_element_type=jnp.float32
)


def normalize(hidden):
    wide = hidden.astype(jnp.float32)
    factor = lax.rsqrt(jnp.mean(wide * wide, axis=-1, keepdims=True) + epsilon)
    return (wide * factor, factor)


def sweep_panel(panel, width):
    rows = lax.broadcasted_iota(jnp.int32, (PANEL, width), 0)
    lanes = lax.broadcasted_iota(jnp.int32, (PANEL, width), 1)
    within = lanes % PANEL
    base = lanes - within
    for k in range(PANEL):
        column = jnp.take_along_axis(panel, base + k, axis=1)
        row = jnp.broadcast_to(panel[k : k + 1, :], (PANEL, width))
        pivot = jnp.broadcast_to(column[k : k + 1, :], (PANEL, width))
        inverse = 1.0 / pivot
        scaled = row * inverse
        inner = panel - column * scaled
        inner = jnp.where(within == k, column * inverse, inner)
        edge = jnp.where(within == k, -inverse, scaled)
        panel = jnp.where(rows == k, edge, inner)
    return panel


def invert_in_place(work, packed, count):
    for start in range(0, count, PACK):
        members = range(start, min(count, start + PACK))
        for k in range(BLOCK // PANEL):
            at = slice(k * PANEL, (k + 1) * PANEL)
            packed[...] = jnp.zeros_like(packed)
            for m in members:
                packed[:, (m - start) * PANEL : (m - start + 1) * PANEL] = work[m, at, at]
            packed[...] = sweep_panel(packed[...], LANES)
            for m in members:
                inverse = -packed[:, (m - start) * PANEL : (m - start + 1) * PANEL]
                row = work[m, at, :]
                across = exact_dot(inverse, row, (((1,), (0,)), ((), ())))
                down = exact_dot(row, inverse, (((0,), (0,)), ((), ())))
                work[m] = work[m] - exact_dot(row, across, (((0,), (0,)), ((), ())))
                work[m, at, :] = across
                work[m, :, at] = down
                work[m, at, at] = -inverse


def invert_kernel(count, blocks_ref, out_ref, work, packed):
    scale = 1.0 / blocks_ref[0, BLOCK : BLOCK + 1, :]
    diagonal = lax.broadcasted_iota(jnp.int32, (BLOCK, BLOCK), 0) == lax.broadcasted_iota(
        jnp.int32, (BLOCK, BLOCK), 1
    )
    for m in range(count):
        work[m] = blocks_ref[m, :BLOCK, :] * scale + jnp.where(diagonal, damping, 0.0)
    invert_in_place(work, packed, count)
    for m in range(count):
        out_ref[m] = (-work[m]).astype(jnp.bfloat16)


def invert_blocks(blocks):
    count = blocks.shape[0]
    shape = (count, BLOCK, BLOCK)
    return pl.pallas_call(
        functools.partial(invert_kernel, count),
        out_shape=jax.ShapeDtypeStruct(shape, jnp.bfloat16),
        in_specs=[pl.BlockSpec(memory_space=pltpu.VMEM)],
        out_specs=pl.BlockSpec(memory_space=pltpu.VMEM),
        scratch_shapes=[
            pltpu.VMEM(shape, jnp.float32),
            pltpu.VMEM((PANEL, LANES), jnp.float32),
        ],
        compiler_params=pltpu.CompilerParams(vmem_limit_bytes=32 * 1024 * 1024),
    )(blocks)


def ring_device(place, count):
    back = lax.div(place, count // 2)
    return (1 - back) * (2 * place) + back * (2 * (count - 1 - place) + 1)


def ring_place(index, count):
    back = lax.rem(index, 2)
    row = lax.div(index, 2)
    return (1 - back) * row + back * (count - 1 - row)


def ring_kernel(count, own_ref, out_ref, local_sem, send_sem, recv_sem):
    rows = own_ref.shape[0]
    first = rows // 32 * 16
    starts, sizes = (0, first), (first, rows - first)
    me = lax.axis_index("dp")
    place = ring_place(me, count)
    targets = [
        ring_device(lax.rem(place + 1, count), count),
        ring_device(lax.rem(place + count - 1, count), count),
    ]
    barrier = pltpu.get_barrier_semaphore()
    for target in targets:
        pl.semaphore_signal(
            barrier, inc=1, device_id={"dp": target}, device_id_type=pl.DeviceIdType.MESH
        )
    pl.semaphore_wait(barrier, 2)

    def part(owner, piece):
        return out_ref.at[pl.ds(pl.multiple_of(owner * rows + starts[piece], 16), sizes[piece])]

    own_copy = pltpu.make_async_copy(
        own_ref, out_ref.at[pl.ds(pl.multiple_of(me * rows, 16), rows)], local_sem
    )
    steps = count // 2
    copies = {}
    waited = set()
    for step in range(steps):
        for piece in range(2):
            for way in range(2):
                if step == steps - 1 and piece != way:
                    continue
                travelled = lax.rem(place + (count - step if way == 0 else step), count)
                owner = ring_device(travelled, count)
                if step == 0:
                    source = own_ref.at[pl.ds(starts[piece], sizes[piece])]
                else:
                    copies[step - 1, piece, way].wait_recv()
                    waited.add((step - 1, piece, way))
                    source = part(owner, piece)
                copy = pltpu.make_async_remote_copy(
                    src_ref=source,
                    dst_ref=part(owner, piece),
                    send_sem=send_sem.at[step, piece, way],
                    recv_sem=recv_sem.at[step, piece, way],
                    device_id={"dp": targets[way]},
                    device_id_type=pl.DeviceIdType.MESH,
                )
                copy.start()
                copies[step, piece, way] = copy
        if step == 0:
            own_copy.start()
    for key, copy in copies.items():
        if key not in waited:
            copy.wait_recv()
    for copy in copies.values():
        copy.wait_send()
    own_copy.wait()


def ring_gather(own, collective_id):
    count = lax.axis_size("dp")
    rows, columns = own.shape
    return pl.pallas_call(
        functools.partial(ring_kernel, count),
        out_shape=jax.ShapeDtypeStruct((count * rows, columns), own.dtype),
        in_specs=[pl.BlockSpec(memory_space=pl.ANY)],
        out_specs=pl.BlockSpec(memory_space=pl.ANY),
        scratch_shapes=[
            pltpu.SemaphoreType.DMA,
            pltpu.SemaphoreType.DMA((count // 2, 2, 2)),
            pltpu.SemaphoreType.DMA((count // 2, 2, 2)),
        ],
        compiler_params=pltpu.CompilerParams(collective_id=collective_id, has_side_effects=True),
    )(own)


def exchange_kernel(
    count, sent_ref, live_ref, out_ref, held, held_live, work, packed, local_sem, send_sem, recv_sem
):
    tokens, columns = held.shape[1:]
    me = lax.axis_index("dp")
    barrier = pltpu.get_barrier_semaphore()
    for offset in range(1, count):
        pl.semaphore_signal(
            barrier,
            inc=1,
            device_id={"dp": lax.rem(me + offset, count)},
            device_id_type=pl.DeviceIdType.MESH,
        )
    pl.semaphore_wait(barrier, count - 1)

    def group(owner):
        kind = lax.div(owner, count // 2)
        column = lax.rem(owner, count // 2) * columns
        return sent_ref.at[kind, :, pl.ds(pl.multiple_of(column, LANES), columns)]

    def remote(source, target, offset, which):
        return pltpu.make_async_remote_copy(
            src_ref=source,
            dst_ref=target,
            send_sem=send_sem.at[offset - 1, which],
            recv_sem=recv_sem.at[offset - 1, which],
            device_id={"dp": lax.rem(me + offset, count)},
            device_id_type=pl.DeviceIdType.MESH,
        )

    copies = {}
    for offset in range(1, count):
        copies[offset, 0] = remote(
            group(lax.rem(me + offset, count)), held.at[me], offset, 0
        )
        copies[offset, 1] = remote(live_ref, held_live.at[me], offset, 1)
        copies[offset, 1].start()
        copies[offset, 0].start()
    own_copy = pltpu.make_async_copy(group(me), held.at[me], local_sem)
    own_copy.start()
    work[...] = jnp.zeros_like(work)
    total = live_ref[...]

    for offset in range(count):
        sender = lax.rem(me + count - offset, count)
        if offset == 0:
            own_copy.wait()
        else:
            copies[offset, 0].wait_recv()
            copies[offset, 1].wait_recv()
            total = total + held_live[sender]
        values = held[sender]
        for m in range(PACK):
            block = values[:, m * BLOCK : (m + 1) * BLOCK]
            work[m] += lax.dot_general(
                block, block, (((0,), (0,)), ((), ())), preferred_element_type=jnp.float32
            )

    scale = 1.0 / total[0:1, 0:1]
    diagonal = lax.broadcasted_iota(jnp.int32, (BLOCK, BLOCK), 0) == lax.broadcasted_iota(
        jnp.int32, (BLOCK, BLOCK), 1
    )
    for m in range(PACK):
        work[m] = work[m] * scale + jnp.where(diagonal, damping, 0.0)
    invert_in_place(work, packed, PACK)
    for m in range(PACK):
        out_ref[:, m * BLOCK : (m + 1) * BLOCK] = (-work[m]).astype(jnp.bfloat16)
    for copy in copies.values():
        copy.wait_send()


def exchange_and_invert(sent, counted, collective_id):
    count = lax.axis_size("dp")
    tokens = sent.shape[1]
    columns = PACK * BLOCK
    return pl.pallas_call(
        functools.partial(exchange_kernel, count),
        out_shape=jax.ShapeDtypeStruct((BLOCK, columns), jnp.bfloat16),
        in_specs=[
            pl.BlockSpec(memory_space=pl.ANY),
            pl.BlockSpec(memory_space=pltpu.VMEM),
        ],
        out_specs=pl.BlockSpec(memory_space=pltpu.VMEM),
        scratch_shapes=[
            pltpu.VMEM((count, tokens, columns), jnp.bfloat16),
            pltpu.VMEM((count, 8, LANES), jnp.float32),
            pltpu.VMEM((PACK, BLOCK, BLOCK), jnp.float32),
            pltpu.VMEM((PANEL, LANES), jnp.float32),
            pltpu.SemaphoreType.DMA,
            pltpu.SemaphoreType.DMA((count - 1, 2)),
            pltpu.SemaphoreType.DMA((count - 1, 2)),
        ],
        compiler_params=pltpu.CompilerParams(
            collective_id=collective_id,
            has_side_effects=True,
            vmem_limit_bytes=32 * 1024 * 1024,
        ),
    )(sent, jnp.full((8, LANES), counted, jnp.float32))


def apply_blocks(values, inverse):
    shaped = values.reshape(values.shape[0], inverse.shape[0], inverse.shape[1])
    result = jnp.einsum("tbi,bij->tbj", shaped, inverse, preferred_element_type=jnp.float32)
    return result.reshape(1, values.shape[0], values.shape[1]).astype(jnp.bfloat16)


def on_device(inputs, cotangent, weights, lengths):
    section_index = lax.axis_index("section")
    section_count = lax.axis_size("section")
    token_count, width = inputs.shape
    micro_count = lengths.shape[0]
    batch_rows = token_count // micro_count
    live = (jnp.arange(batch_rows)[None, :] < lengths[:, None]).reshape(token_count, 1)
    counted = jnp.sum(live.astype(jnp.float32))
    full_weight = ring_gather(weights[0], 0)

    hidden = inputs
    for stage in range(section_count - 1):
        activation = normalize(hidden)[0].astype(jnp.bfloat16)
        result = (
            hidden.astype(jnp.float32)
            + jnp.dot(activation, full_weight, preferred_element_type=jnp.float32)
        ).astype(jnp.bfloat16)
        arrived = lax.ppermute(result, "section", [(stage, stage + 1)])
        hidden = jnp.where(section_index == stage + 1, arrived, hidden)

    normed, factor = normalize(hidden)
    activations = normed.astype(jnp.bfloat16)
    gradients = cotangent
    for stage in range(section_count - 1, 0, -1):
        back = lax.dot_general(
            gradients, full_weight, (((1,), (1,)), ((), ())), preferred_element_type=jnp.float32
        )
        through = factor * (back - normed * jnp.mean(back * normed, axis=-1, keepdims=True))
        result = (gradients.astype(jnp.float32) + through).astype(jnp.bfloat16)
        arrived = lax.ppermute(result, "section", [(stage, stage - 1)])
        gradients = jnp.where(section_index == stage - 1, arrived, gradients)

    blocks_each = width // BLOCK
    zero_value = jnp.zeros((), jnp.bfloat16)
    dp_count = lax.axis_size("dp")
    if 2 * blocks_each == PACK * dp_count and dp_count % 2 == 0:
        sent = jnp.where(live[None], jnp.stack([activations, gradients]), zero_value)
        inverse = exchange_and_invert(sent, counted, 2)
        inverses = ring_gather(inverse, 1).reshape(dp_count, BLOCK, PACK, BLOCK)
        inverses = jnp.swapaxes(inverses, 1, 2).reshape(-1, BLOCK, BLOCK)
    else:
        masked_act = jnp.where(live, activations, zero_value).reshape(token_count, blocks_each, BLOCK)
        masked_grad = jnp.where(live, gradients, zero_value).reshape(token_count, blocks_each, BLOCK)
        gram_act = jnp.einsum(
            "tbi,tbj->bij", masked_act, masked_act, preferred_element_type=jnp.float32
        )
        gram_grad = jnp.einsum(
            "tbi,tbj->bij", masked_grad, masked_grad, preferred_element_type=jnp.float32
        )
        stacked = jnp.concatenate([gram_act, gram_grad], axis=0)
        counts = jnp.full((stacked.shape[0], 8, BLOCK), counted, jnp.float32)
        stacked = jnp.concatenate([stacked, counts], axis=1)
        owned = lax.psum_scatter(stacked, "dp", scatter_dimension=0, tiled=True)
        inverse = invert_blocks(owned)
        inverses = ring_gather(inverse.reshape(-1, BLOCK), 1).reshape(-1, BLOCK, BLOCK)
    pre_inputs = apply_blocks(activations, inverses[:blocks_each])
    pre_grads = apply_blocks(gradients, inverses[blocks_each:])
    return (pre_inputs, pre_grads)


def solution(mesh):
    in_specs = (P("dp", None), P("dp", None), P("section", "dp", None), P("dp"))
    out_specs = (P("section", "dp", None), P("section", "dp", None))
    return jax.shard_map(
        on_device, mesh=mesh, in_specs=in_specs, out_specs=out_specs, check_vma=False
    )
```

```python
import functools

import jax
import jax.numpy as jnp
from jax import lax
from jax.experimental import pallas as pl
from jax.experimental.pallas import tpu as pltpu
from jax.sharding import PartitionSpec as P

BLOCK = 160
PANEL = 32
LANES = 128
PACK = LANES // PANEL

epsilon = 1e-05
damping = 0.1

exact_dot = functools.partial(
    lax.dot_general, precision=lax.Precision.HIGHEST, preferred_element_type=jnp.float32
)


def normalize(hidden):
    wide = hidden.astype(jnp.float32)
    factor = lax.rsqrt(jnp.mean(wide * wide, axis=-1, keepdims=True) + epsilon)
    return (wide * factor, factor)


def sweep_panel(panel, width):
    rows = lax.broadcasted_iota(jnp.int32, (PANEL, width), 0)
    lanes = lax.broadcasted_iota(jnp.int32, (PANEL, width), 1)
    within = lanes % PANEL
    base = lanes - within
    for k in range(PANEL):
        column = jnp.take_along_axis(panel, base + k, axis=1)
        row = jnp.broadcast_to(panel[k : k + 1, :], (PANEL, width))
        pivot = jnp.broadcast_to(column[k : k + 1, :], (PANEL, width))
        inverse = 1.0 / pivot
        scaled = row * inverse
        inner = panel - column * scaled
        inner = jnp.where(within == k, column * inverse, inner)
        edge = jnp.where(within == k, -inverse, scaled)
        panel = jnp.where(rows == k, edge, inner)
    return panel


def invert_in_place(work, packed, count):
    for start in range(0, count, PACK):
        members = range(start, min(count, start + PACK))
        for k in range(BLOCK // PANEL):
            at = slice(k * PANEL, (k + 1) * PANEL)
            packed[...] = jnp.zeros_like(packed)
            for m in members:
                packed[:, (m - start) * PANEL : (m - start + 1) * PANEL] = work[m, at, at]
            packed[...] = sweep_panel(packed[...], LANES)
            for m in members:
                inverse = -packed[:, (m - start) * PANEL : (m - start + 1) * PANEL]
                row = work[m, at, :]
                across = exact_dot(inverse, row, (((1,), (0,)), ((), ())))
                down = exact_dot(row, inverse, (((0,), (0,)), ((), ())))
                work[m] = work[m] - exact_dot(row, across, (((0,), (0,)), ((), ())))
                work[m, at, :] = across
                work[m, :, at] = down
                work[m, at, at] = -inverse


def invert_kernel(count, blocks_ref, out_ref, work, packed):
    scale = 1.0 / blocks_ref[0, BLOCK : BLOCK + 1, :]
    diagonal = lax.broadcasted_iota(jnp.int32, (BLOCK, BLOCK), 0) == lax.broadcasted_iota(
        jnp.int32, (BLOCK, BLOCK), 1
    )
    for m in range(count):
        work[m] = blocks_ref[m, :BLOCK, :] * scale + jnp.where(diagonal, damping, 0.0)
    invert_in_place(work, packed, count)
    for m in range(count):
        out_ref[m] = (-work[m]).astype(jnp.bfloat16)


def invert_blocks(blocks):
    count = blocks.shape[0]
    shape = (count, BLOCK, BLOCK)
    return pl.pallas_call(
        functools.partial(invert_kernel, count),
        out_shape=jax.ShapeDtypeStruct(shape, jnp.bfloat16),
        in_specs=[pl.BlockSpec(memory_space=pltpu.VMEM)],
        out_specs=pl.BlockSpec(memory_space=pltpu.VMEM),
        scratch_shapes=[
            pltpu.VMEM(shape, jnp.float32),
            pltpu.VMEM((PANEL, LANES), jnp.float32),
        ],
        compiler_params=pltpu.CompilerParams(vmem_limit_bytes=32 * 1024 * 1024),
    )(blocks)


def ring_device(place, count):
    back = lax.div(place, count // 2)
    return (1 - back) * (2 * place) + back * (2 * (count - 1 - place) + 1)


def ring_place(index, count):
    back = lax.rem(index, 2)
    row = lax.div(index, 2)
    return (1 - back) * row + back * (count - 1 - row)


def ring_kernel(count, own_ref, out_ref, local_sem, send_sem, recv_sem):
    rows = own_ref.shape[0]
    first = rows // 32 * 16
    starts, sizes = (0, first), (first, rows - first)
    me = lax.axis_index("dp")
    place = ring_place(me, count)
    targets = [
        ring_device(lax.rem(place + 1, count), count),
        ring_device(lax.rem(place + count - 1, count), count),
    ]
    barrier = pltpu.get_barrier_semaphore()
    for target in targets:
        pl.semaphore_signal(
            barrier, inc=1, device_id={"dp": target}, device_id_type=pl.DeviceIdType.MESH
        )
    pl.semaphore_wait(barrier, 2)

    def part(owner, piece):
        return out_ref.at[pl.ds(pl.multiple_of(owner * rows + starts[piece], 16), sizes[piece])]

    own_copy = pltpu.make_async_copy(
        own_ref, out_ref.at[pl.ds(pl.multiple_of(me * rows, 16), rows)], local_sem
    )
    steps = count // 2
    copies = {}
    waited = set()
    for step in range(steps):
        for piece in range(2):
            for way in range(2):
                if step == steps - 1 and piece != way:
                    continue
                travelled = lax.rem(place + (count - step if way == 0 else step), count)
                owner = ring_device(travelled, count)
                if step == 0:
                    source = own_ref.at[pl.ds(starts[piece], sizes[piece])]
                else:
                    copies[step - 1, piece, way].wait_recv()
                    waited.add((step - 1, piece, way))
                    source = part(owner, piece)
                copy = pltpu.make_async_remote_copy(
                    src_ref=source,
                    dst_ref=part(owner, piece),
                    send_sem=send_sem.at[step, piece, way],
                    recv_sem=recv_sem.at[step, piece, way],
                    device_id={"dp": targets[way]},
                    device_id_type=pl.DeviceIdType.MESH,
                )
                copy.start()
                copies[step, piece, way] = copy
        if step == 0:
            own_copy.start()
    for key, copy in copies.items():
        if key not in waited:
            copy.wait_recv()
    for copy in copies.values():
        copy.wait_send()
    own_copy.wait()


def ring_gather(own, collective_id):
    count = lax.axis_size("dp")
    rows, columns = own.shape
    return pl.pallas_call(
        functools.partial(ring_kernel, count),
        out_shape=jax.ShapeDtypeStruct((count * rows, columns), own.dtype),
        in_specs=[pl.BlockSpec(memory_space=pl.ANY)],
        out_specs=pl.BlockSpec(memory_space=pl.ANY),
        scratch_shapes=[
            pltpu.SemaphoreType.DMA,
            pltpu.SemaphoreType.DMA((count // 2, 2, 2)),
            pltpu.SemaphoreType.DMA((count // 2, 2, 2)),
        ],
        compiler_params=pltpu.CompilerParams(collective_id=collective_id, has_side_effects=True),
    )(own)


def exchange_kernel(
    count, sent_ref, live_ref, out_ref, held, held_live, work, packed, local_sem, send_sem, recv_sem
):
    tokens, columns = held.shape[1:]
    me = lax.axis_index("dp")
    barrier = pltpu.get_barrier_semaphore()
    for offset in range(1, count):
        pl.semaphore_signal(
            barrier,
            inc=1,
            device_id={"dp": lax.rem(me + offset, count)},
            device_id_type=pl.DeviceIdType.MESH,
        )
    pl.semaphore_wait(barrier, count - 1)

    def group(owner):
        kind = lax.div(owner, count // 2)
        column = lax.rem(owner, count // 2) * columns
        return sent_ref.at[kind, :, pl.ds(pl.multiple_of(column, LANES), columns)]

    def remote(source, target, offset, which):
        return pltpu.make_async_remote_copy(
            src_ref=source,
            dst_ref=target,
            send_sem=send_sem.at[offset - 1, which],
            recv_sem=recv_sem.at[offset - 1, which],
            device_id={"dp": lax.rem(me + offset, count)},
            device_id_type=pl.DeviceIdType.MESH,
        )

    copies = {}
    for offset in range(1, count):
        copies[offset, 0] = remote(
            group(lax.rem(me + offset, count)), held.at[me], offset, 0
        )
        copies[offset, 1] = remote(live_ref, held_live.at[me], offset, 1)
        copies[offset, 1].start()
        copies[offset, 0].start()
    own_copy = pltpu.make_async_copy(group(me), held.at[me], local_sem)
    own_copy.start()
    work[...] = jnp.zeros_like(work)
    total = live_ref[...]

    for offset in range(count):
        sender = lax.rem(me + count - offset, count)
        if offset == 0:
            own_copy.wait()
        else:
            copies[offset, 0].wait_recv()
            copies[offset, 1].wait_recv()
            total = total + held_live[sender]
        values = held[sender]
        for m in range(PACK):
            block = values[:, m * BLOCK : (m + 1) * BLOCK]
            work[m] += lax.dot_general(
                block, block, (((0,), (0,)), ((), ())), preferred_element_type=jnp.float32
            )

    scale = 1.0 / total[0:1, 0:1]
    diagonal = lax.broadcasted_iota(jnp.int32, (BLOCK, BLOCK), 0) == lax.broadcasted_iota(
        jnp.int32, (BLOCK, BLOCK), 1
    )
    for m in range(PACK):
        work[m] = work[m] * scale + jnp.where(diagonal, damping, 0.0)
    invert_in_place(work, packed, PACK)
    for m in range(PACK):
        out_ref[:, m * BLOCK : (m + 1) * BLOCK] = (-work[m]).astype(jnp.bfloat16)
    for copy in copies.values():
        copy.wait_send()


def exchange_and_invert(sent, counted, collective_id):
    count = lax.axis_size("dp")
    tokens = sent.shape[1]
    columns = PACK * BLOCK
    return pl.pallas_call(
        functools.partial(exchange_kernel, count),
        out_shape=jax.ShapeDtypeStruct((BLOCK, columns), jnp.bfloat16),
        in_specs=[
            pl.BlockSpec(memory_space=pl.ANY),
            pl.BlockSpec(memory_space=pltpu.VMEM),
        ],
        out_specs=pl.BlockSpec(memory_space=pltpu.VMEM),
        scratch_shapes=[
            pltpu.VMEM((count, tokens, columns), jnp.bfloat16),
            pltpu.VMEM((count, 8, LANES), jnp.float32),
            pltpu.VMEM((PACK, BLOCK, BLOCK), jnp.float32),
            pltpu.VMEM((PANEL, LANES), jnp.float32),
            pltpu.SemaphoreType.DMA,
            pltpu.SemaphoreType.DMA((count - 1, 2)),
            pltpu.SemaphoreType.DMA((count - 1, 2)),
        ],
        compiler_params=pltpu.CompilerParams(
            collective_id=collective_id,
            has_side_effects=True,
            vmem_limit_bytes=32 * 1024 * 1024,
        ),
    )(sent, jnp.full((8, LANES), counted, jnp.float32))


def apply_kernel(act_ref, grad_ref, act_inverse_ref, grad_inverse_ref, first_ref, second_ref):
    for values, inverse, result in (
        (act_ref, act_inverse_ref, first_ref),
        (grad_ref, grad_inverse_ref, second_ref),
    ):
        for m in range(PACK):
            at = slice(m * BLOCK, (m + 1) * BLOCK)
            result[0, :, at] = jnp.dot(
                values[:, at], inverse[:, at], preferred_element_type=jnp.float32
            ).astype(jnp.bfloat16)


def apply_groups(activations, gradients, inverses):
    tokens, width = activations.shape
    columns = PACK * BLOCK
    groups = width // columns
    values = pl.BlockSpec((tokens, columns), lambda g: (0, g))
    result = pl.BlockSpec((1, tokens, columns), lambda g: (0, 0, g))
    shape = jax.ShapeDtypeStruct((1, tokens, width), jnp.bfloat16)
    return pl.pallas_call(
        apply_kernel,
        grid=(groups,),
        out_shape=(shape, shape),
        in_specs=[
            values,
            values,
            pl.BlockSpec((BLOCK, columns), lambda g: (g, 0)),
            pl.BlockSpec((BLOCK, columns), lambda g: (g + groups, 0)),
        ],
        out_specs=(result, result),
        compiler_params=pltpu.CompilerParams(vmem_limit_bytes=32 * 1024 * 1024),
    )(activations, gradients, inverses, inverses)


def apply_blocks(values, inverse):
    shaped = values.reshape(values.shape[0], inverse.shape[0], inverse.shape[1])
    result = jnp.einsum("tbi,bij->tbj", shaped, inverse, preferred_element_type=jnp.float32)
    return result.reshape(1, values.shape[0], values.shape[1]).astype(jnp.bfloat16)


def on_device(inputs, cotangent, weights, lengths):
    section_index = lax.axis_index("section")
    section_count = lax.axis_size("section")
    token_count, width = inputs.shape
    micro_count = lengths.shape[0]
    batch_rows = token_count // micro_count
    live = (jnp.arange(batch_rows)[None, :] < lengths[:, None]).reshape(token_count, 1)
    counted = jnp.sum(live.astype(jnp.float32))
    full_weight = ring_gather(weights[0], 0)

    hidden = inputs
    for stage in range(section_count - 1):
        activation = normalize(hidden)[0].astype(jnp.bfloat16)
        result = (
            hidden.astype(jnp.float32)
            + jnp.dot(activation, full_weight, preferred_element_type=jnp.float32)
        ).astype(jnp.bfloat16)
        arrived = lax.ppermute(result, "section", [(stage, stage + 1)])
        hidden = jnp.where(section_index == stage + 1, arrived, hidden)

    normed, factor = normalize(hidden)
    activations = normed.astype(jnp.bfloat16)
    gradients = cotangent
    for stage in range(section_count - 1, 0, -1):
        back = lax.dot_general(
            gradients, full_weight, (((1,), (1,)), ((), ())), preferred_element_type=jnp.float32
        )
        through = factor * (back - normed * jnp.mean(back * normed, axis=-1, keepdims=True))
        result = (gradients.astype(jnp.float32) + through).astype(jnp.bfloat16)
        arrived = lax.ppermute(result, "section", [(stage, stage - 1)])
        gradients = jnp.where(section_index == stage - 1, arrived, gradients)

    blocks_each = width // BLOCK
    zero_value = jnp.zeros((), jnp.bfloat16)
    dp_count = lax.axis_size("dp")
    if 2 * blocks_each == PACK * dp_count and dp_count % 2 == 0:
        sent = jnp.where(live[None], jnp.stack([activations, gradients]), zero_value)
        inverse = exchange_and_invert(sent, counted, 2)
        return apply_groups(activations, gradients, ring_gather(inverse, 1))
    else:
        masked_act = jnp.where(live, activations, zero_value).reshape(token_count, blocks_each, BLOCK)
        masked_grad = jnp.where(live, gradients, zero_value).reshape(token_count, blocks_each, BLOCK)
        gram_act = jnp.einsum(
            "tbi,tbj->bij", masked_act, masked_act, preferred_element_type=jnp.float32
        )
        gram_grad = jnp.einsum(
            "tbi,tbj->bij", masked_grad, masked_grad, preferred_element_type=jnp.float32
        )
        stacked = jnp.concatenate([gram_act, gram_grad], axis=0)
        counts = jnp.full((stacked.shape[0], 8, BLOCK), counted, jnp.float32)
        stacked = jnp.concatenate([stacked, counts], axis=1)
        owned = lax.psum_scatter(stacked, "dp", scatter_dimension=0, tiled=True)
        inverse = invert_blocks(owned)
        inverses = ring_gather(inverse.reshape(-1, BLOCK), 1).reshape(-1, BLOCK, BLOCK)
    pre_inputs = apply_blocks(activations, inverses[:blocks_each])
    pre_grads = apply_blocks(gradients, inverses[blocks_each:])
    return (pre_inputs, pre_grads)


def solution(mesh):
    in_specs = (P("dp", None), P("dp", None), P("section", "dp", None), P("dp"))
    out_specs = (P("section", "dp", None), P("section", "dp", None))
    return jax.shard_map(
        on_device, mesh=mesh, in_specs=in_specs, out_specs=out_specs, check_vma=False
    )
```

```python
import functools

import jax
import jax.numpy as jnp
from jax import lax
from jax.experimental import pallas as pl
from jax.experimental.pallas import tpu as pltpu
from jax.sharding import PartitionSpec as P

BLOCK = 160
PANEL = 32
LANES = 128
PACK = LANES // PANEL

epsilon = 1e-05
damping = 0.1

exact_dot = functools.partial(
    lax.dot_general, precision=lax.Precision.HIGHEST, preferred_element_type=jnp.float32
)


def normalize(hidden):
    wide = hidden.astype(jnp.float32)
    factor = lax.rsqrt(jnp.mean(wide * wide, axis=-1, keepdims=True) + epsilon)
    return (wide * factor, factor)


def sweep_panel(panel, width):
    rows = lax.broadcasted_iota(jnp.int32, (PANEL, width), 0)
    lanes = lax.broadcasted_iota(jnp.int32, (PANEL, width), 1)
    within = lanes % PANEL
    base = lanes - within
    for k in range(PANEL):
        column = jnp.take_along_axis(panel, base + k, axis=1)
        row = jnp.broadcast_to(panel[k : k + 1, :], (PANEL, width))
        pivot = jnp.broadcast_to(column[k : k + 1, :], (PANEL, width))
        inverse = 1.0 / pivot
        scaled = row * inverse
        inner = panel - column * scaled
        inner = jnp.where(within == k, column * inverse, inner)
        edge = jnp.where(within == k, -inverse, scaled)
        panel = jnp.where(rows == k, edge, inner)
    return panel


def invert_in_place(work, packed, count):
    for start in range(0, count, PACK):
        members = range(start, min(count, start + PACK))
        for k in range(BLOCK // PANEL):
            at = slice(k * PANEL, (k + 1) * PANEL)
            packed[...] = jnp.zeros_like(packed)
            for m in members:
                packed[:, (m - start) * PANEL : (m - start + 1) * PANEL] = work[m, at, at]
            packed[...] = sweep_panel(packed[...], LANES)
            for m in members:
                inverse = -packed[:, (m - start) * PANEL : (m - start + 1) * PANEL]
                row = work[m, at, :]
                across = exact_dot(inverse, row, (((1,), (0,)), ((), ())))
                down = exact_dot(row, inverse, (((0,), (0,)), ((), ())))
                work[m] = work[m] - exact_dot(row, across, (((0,), (0,)), ((), ())))
                work[m, at, :] = across
                work[m, :, at] = down
                work[m, at, at] = -inverse


def invert_kernel(count, blocks_ref, out_ref, work, packed):
    scale = 1.0 / blocks_ref[0, BLOCK : BLOCK + 1, :]
    diagonal = lax.broadcasted_iota(jnp.int32, (BLOCK, BLOCK), 0) == lax.broadcasted_iota(
        jnp.int32, (BLOCK, BLOCK), 1
    )
    for m in range(count):
        work[m] = blocks_ref[m, :BLOCK, :] * scale + jnp.where(diagonal, damping, 0.0)
    invert_in_place(work, packed, count)
    for m in range(count):
        out_ref[m] = (-work[m]).astype(jnp.bfloat16)


def invert_blocks(blocks):
    count = blocks.shape[0]
    shape = (count, BLOCK, BLOCK)
    return pl.pallas_call(
        functools.partial(invert_kernel, count),
        out_shape=jax.ShapeDtypeStruct(shape, jnp.bfloat16),
        in_specs=[pl.BlockSpec(memory_space=pltpu.VMEM)],
        out_specs=pl.BlockSpec(memory_space=pltpu.VMEM),
        scratch_shapes=[
            pltpu.VMEM(shape, jnp.float32),
            pltpu.VMEM((PANEL, LANES), jnp.float32),
        ],
        compiler_params=pltpu.CompilerParams(vmem_limit_bytes=32 * 1024 * 1024),
    )(blocks)


def ring_device(place, count):
    back = lax.div(place, count // 2)
    return (1 - back) * (2 * place) + back * (2 * (count - 1 - place) + 1)


def ring_place(index, count):
    back = lax.rem(index, 2)
    row = lax.div(index, 2)
    return (1 - back) * row + back * (count - 1 - row)


def ring_kernel(count, own_ref, out_ref, local_sem, send_sem, recv_sem):
    rows = own_ref.shape[0]
    first = rows // 32 * 16
    starts, sizes = (0, first), (first, rows - first)
    me = lax.axis_index("dp")
    place = ring_place(me, count)
    targets = [
        ring_device(lax.rem(place + 1, count), count),
        ring_device(lax.rem(place + count - 1, count), count),
    ]
    barrier = pltpu.get_barrier_semaphore()
    for target in targets:
        pl.semaphore_signal(
            barrier, inc=1, device_id={"dp": target}, device_id_type=pl.DeviceIdType.MESH
        )
    pl.semaphore_wait(barrier, 2)

    def part(owner, piece):
        return out_ref.at[pl.ds(pl.multiple_of(owner * rows + starts[piece], 16), sizes[piece])]

    own_copy = pltpu.make_async_copy(
        own_ref, out_ref.at[pl.ds(pl.multiple_of(me * rows, 16), rows)], local_sem
    )
    steps = count // 2
    copies = {}
    waited = set()
    for step in range(steps):
        for piece in range(2):
            for way in range(2):
                if step == steps - 1 and piece != way:
                    continue
                travelled = lax.rem(place + (count - step if way == 0 else step), count)
                owner = ring_device(travelled, count)
                if step == 0:
                    source = own_ref.at[pl.ds(starts[piece], sizes[piece])]
                else:
                    copies[step - 1, piece, way].wait_recv()
                    waited.add((step - 1, piece, way))
                    source = part(owner, piece)
                copy = pltpu.make_async_remote_copy(
                    src_ref=source,
                    dst_ref=part(owner, piece),
                    send_sem=send_sem.at[step, piece, way],
                    recv_sem=recv_sem.at[step, piece, way],
                    device_id={"dp": targets[way]},
                    device_id_type=pl.DeviceIdType.MESH,
                )
                copy.start()
                copies[step, piece, way] = copy
        if step == 0:
            own_copy.start()
    for key, copy in copies.items():
        if key not in waited:
            copy.wait_recv()
    for copy in copies.values():
        copy.wait_send()
    own_copy.wait()


def ring_gather(own, collective_id, space=pl.ANY):
    count = lax.axis_size("dp")
    rows, columns = own.shape
    return pl.pallas_call(
        functools.partial(ring_kernel, count),
        out_shape=jax.ShapeDtypeStruct((count * rows, columns), own.dtype),
        in_specs=[pl.BlockSpec(memory_space=space)],
        out_specs=pl.BlockSpec(memory_space=space),
        scratch_shapes=[
            pltpu.SemaphoreType.DMA,
            pltpu.SemaphoreType.DMA((count // 2, 2, 2)),
            pltpu.SemaphoreType.DMA((count // 2, 2, 2)),
        ],
        compiler_params=pltpu.CompilerParams(collective_id=collective_id, has_side_effects=True),
    )(own)


def exchange_kernel(
    count, sent_ref, live_ref, out_ref, held, held_live, work, packed, local_sem, send_sem, recv_sem
):
    tokens, columns = held.shape[1:]
    me = lax.axis_index("dp")
    barrier = pltpu.get_barrier_semaphore()
    for offset in range(1, count):
        pl.semaphore_signal(
            barrier,
            inc=1,
            device_id={"dp": lax.rem(me + offset, count)},
            device_id_type=pl.DeviceIdType.MESH,
        )
    pl.semaphore_wait(barrier, count - 1)

    def group(owner):
        kind = lax.div(owner, count // 2)
        column = lax.rem(owner, count // 2) * columns
        return sent_ref.at[kind, :, pl.ds(pl.multiple_of(column, LANES), columns)]

    def remote(source, target, offset, which):
        return pltpu.make_async_remote_copy(
            src_ref=source,
            dst_ref=target,
            send_sem=send_sem.at[offset - 1, which],
            recv_sem=recv_sem.at[offset - 1, which],
            device_id={"dp": lax.rem(me + offset, count)},
            device_id_type=pl.DeviceIdType.MESH,
        )

    copies = {}
    for offset in range(1, count):
        copies[offset, 0] = remote(
            group(lax.rem(me + offset, count)), held.at[me], offset, 0
        )
        copies[offset, 1] = remote(live_ref, held_live.at[me], offset, 1)
        copies[offset, 1].start()
        copies[offset, 0].start()
    own_copy = pltpu.make_async_copy(group(me), held.at[me], local_sem)
    own_copy.start()
    work[...] = jnp.zeros_like(work)
    total = live_ref[...]

    for offset in range(count):
        sender = lax.rem(me + count - offset, count)
        if offset == 0:
            own_copy.wait()
        else:
            copies[offset, 0].wait_recv()
            copies[offset, 1].wait_recv()
            total = total + held_live[sender]
        values = held[sender]
        for m in range(PACK):
            block = values[:, m * BLOCK : (m + 1) * BLOCK]
            work[m] += lax.dot_general(
                block, block, (((0,), (0,)), ((), ())), preferred_element_type=jnp.float32
            )

    scale = 1.0 / total[0:1, 0:1]
    diagonal = lax.broadcasted_iota(jnp.int32, (BLOCK, BLOCK), 0) == lax.broadcasted_iota(
        jnp.int32, (BLOCK, BLOCK), 1
    )
    for m in range(PACK):
        work[m] = work[m] * scale + jnp.where(diagonal, damping, 0.0)
    invert_in_place(work, packed, PACK)
    for m in range(PACK):
        out_ref[:, m * BLOCK : (m + 1) * BLOCK] = (-work[m]).astype(jnp.bfloat16)
    for copy in copies.values():
        copy.wait_send()


def exchange_and_invert(sent, counted, collective_id):
    count = lax.axis_size("dp")
    tokens = sent.shape[1]
    columns = PACK * BLOCK
    return pl.pallas_call(
        functools.partial(exchange_kernel, count),
        out_shape=jax.ShapeDtypeStruct((BLOCK, columns), jnp.bfloat16),
        in_specs=[
            pl.BlockSpec(memory_space=pl.ANY),
            pl.BlockSpec(memory_space=pltpu.VMEM),
        ],
        out_specs=pl.BlockSpec(memory_space=pltpu.VMEM),
        scratch_shapes=[
            pltpu.VMEM((count, tokens, columns), jnp.bfloat16),
            pltpu.VMEM((count, 8, LANES), jnp.float32),
            pltpu.VMEM((PACK, BLOCK, BLOCK), jnp.float32),
            pltpu.VMEM((PANEL, LANES), jnp.float32),
            pltpu.SemaphoreType.DMA,
            pltpu.SemaphoreType.DMA((count - 1, 2)),
            pltpu.SemaphoreType.DMA((count - 1, 2)),
        ],
        compiler_params=pltpu.CompilerParams(
            collective_id=collective_id,
            has_side_effects=True,
            vmem_limit_bytes=32 * 1024 * 1024,
        ),
    )(sent, jnp.full((8, LANES), counted, jnp.float32))


def apply_kernel(act_ref, grad_ref, act_inverse_ref, grad_inverse_ref, first_ref, second_ref):
    for values, inverse, result in (
        (act_ref, act_inverse_ref, first_ref),
        (grad_ref, grad_inverse_ref, second_ref),
    ):
        for m in range(PACK):
            at = slice(m * BLOCK, (m + 1) * BLOCK)
            result[0, :, at] = jnp.dot(
                values[:, at], inverse[:, at], preferred_element_type=jnp.float32
            ).astype(jnp.bfloat16)


def apply_groups(activations, gradients, inverses):
    tokens, width = activations.shape
    columns = PACK * BLOCK
    groups = width // columns
    values = pl.BlockSpec((tokens, columns), lambda g: (0, g))
    result = pl.BlockSpec((1, tokens, columns), lambda g: (0, 0, g))
    shape = jax.ShapeDtypeStruct((1, tokens, width), jnp.bfloat16)
    return pl.pallas_call(
        apply_kernel,
        grid=(groups,),
        out_shape=(shape, shape),
        in_specs=[
            values,
            values,
            pl.BlockSpec((BLOCK, columns), lambda g: (g, 0)),
            pl.BlockSpec((BLOCK, columns), lambda g: (g + groups, 0)),
        ],
        out_specs=(result, result),
        compiler_params=pltpu.CompilerParams(vmem_limit_bytes=32 * 1024 * 1024),
    )(activations, gradients, inverses, inverses)


def apply_blocks(values, inverse):
    shaped = values.reshape(values.shape[0], inverse.shape[0], inverse.shape[1])
    result = jnp.einsum("tbi,bij->tbj", shaped, inverse, preferred_element_type=jnp.float32)
    return result.reshape(1, values.shape[0], values.shape[1]).astype(jnp.bfloat16)


def on_device(inputs, cotangent, weights, lengths):
    section_index = lax.axis_index("section")
    section_count = lax.axis_size("section")
    token_count, width = inputs.shape
    micro_count = lengths.shape[0]
    batch_rows = token_count // micro_count
    live = (jnp.arange(batch_rows)[None, :] < lengths[:, None]).reshape(token_count, 1)
    counted = jnp.sum(live.astype(jnp.float32))
    full_weight = ring_gather(weights[0], 0)

    hidden = inputs
    for stage in range(section_count - 1):
        activation = normalize(hidden)[0].astype(jnp.bfloat16)
        result = (
            hidden.astype(jnp.float32)
            + jnp.dot(activation, full_weight, preferred_element_type=jnp.float32)
        ).astype(jnp.bfloat16)
        arrived = lax.ppermute(result, "section", [(stage, stage + 1)])
        hidden = jnp.where(section_index == stage + 1, arrived, hidden)

    normed, factor = normalize(hidden)
    activations = normed.astype(jnp.bfloat16)
    gradients = cotangent
    for stage in range(section_count - 1, 0, -1):
        back = lax.dot_general(
            gradients, full_weight, (((1,), (1,)), ((), ())), preferred_element_type=jnp.float32
        )
        through = factor * (back - normed * jnp.mean(back * normed, axis=-1, keepdims=True))
        result = (gradients.astype(jnp.float32) + through).astype(jnp.bfloat16)
        arrived = lax.ppermute(result, "section", [(stage, stage - 1)])
        gradients = jnp.where(section_index == stage - 1, arrived, gradients)

    blocks_each = width // BLOCK
    zero_value = jnp.zeros((), jnp.bfloat16)
    dp_count = lax.axis_size("dp")
    if 2 * blocks_each == PACK * dp_count and dp_count % 2 == 0:
        sent = jnp.where(live[None], jnp.stack([activations, gradients]), zero_value)
        inverse = exchange_and_invert(sent, counted, 2)
        return apply_groups(activations, gradients, ring_gather(inverse, 1, pltpu.VMEM))
    else:
        masked_act = jnp.where(live, activations, zero_value).reshape(token_count, blocks_each, BLOCK)
        masked_grad = jnp.where(live, gradients, zero_value).reshape(token_count, blocks_each, BLOCK)
        gram_act = jnp.einsum(
            "tbi,tbj->bij", masked_act, masked_act, preferred_element_type=jnp.float32
        )
        gram_grad = jnp.einsum(
            "tbi,tbj->bij", masked_grad, masked_grad, preferred_element_type=jnp.float32
        )
        stacked = jnp.concatenate([gram_act, gram_grad], axis=0)
        counts = jnp.full((stacked.shape[0], 8, BLOCK), counted, jnp.float32)
        stacked = jnp.concatenate([stacked, counts], axis=1)
        owned = lax.psum_scatter(stacked, "dp", scatter_dimension=0, tiled=True)
        inverse = invert_blocks(owned)
        inverses = ring_gather(inverse.reshape(-1, BLOCK), 1).reshape(-1, BLOCK, BLOCK)
    pre_inputs = apply_blocks(activations, inverses[:blocks_each])
    pre_grads = apply_blocks(gradients, inverses[blocks_each:])
    return (pre_inputs, pre_grads)


def solution(mesh):
    in_specs = (P("dp", None), P("dp", None), P("section", "dp", None), P("dp"))
    out_specs = (P("section", "dp", None), P("section", "dp", None))
    return jax.shard_map(
        on_device, mesh=mesh, in_specs=in_specs, out_specs=out_specs, check_vma=False
    )
```
